32 devices in a mesh: group: 2 (over x), row: 16 (over z, y, core).
Axes of the slice: x: 2, y: 2, z: 4, core: 2. Of those that a mesh axis runs over, the one named last changes fastest.
Arguments:
- features: float32 [8192, 128], P(('group', 'row')), parts along dimension 0, may hold values from -90 to 90
- w_left: float32 [128, 512], replicated, may hold values from -0.5 to 0.5
- w_right: float32 [128, 512], replicated, may hold values from -0.5 to 0.5
- attention: float32 [8, 64], replicated, may hold values from -0.75 to 0.75
- requests: int32 [32, 16], P(('group', 'row')), parts along dimension 0, may hold values from -1 to 7, as said below
- src_slot: int32 [8192, 8], P(('group', 'row')), parts along dimension 0, may hold values from 0 to 511, as said below
- edge_mask: int32 [8192, 8], P(('group', 'row')), parts along dimension 0, may hold values from 0 to 1, as said below
- g_out: float32 [8192, 512], P(('group', 'row')), parts along dimension 0, may hold values from -6 to 6
Outputs:
- out: float32 [8192, 512], P(('group', 'row')), parts along dimension 0
- feature_gradient: float32 [8192, 128], P(('group', 'row')), parts along dimension 0
- grad_left: float32 [256, 512], P('group'), parts along dimension 0
- grad_right: float32 [256, 512], P('group'), parts along dimension 0
- grad_att: float32 [16, 64], P('group'), parts along dimension 0
The draws below stay inside these ranges and needn't reach their ends.
There are 2 independent parts, one for each index of `group`. The reference program is written for one: setup_inputs(seed, part) draws one part's arguments, and reference() takes and returns one part's arrays. A program takes and returns all parts, laid end to end along the dimension named above; an argument that names none is the same for every part. Nothing has to cross between parts.
Inputs may be any that keep to these rules, and one draw needn't show every extreme that they name: `requests`: each device reads at most one tile of each device. `src_slot`: every entry names a slot p * 32 + r whose request requests[d, p] on the destination's device d is not -1. `edge_mask`: the first slot of every row is live.
All inputs are finite; a program needn't handle non-finite values.
Results may differ from the reference program's by a relative error of at most 0.007.
Values sent between devices are 32-bit elements; how exact they have to be, the bound alone decides.
A program may use at most 128 MiB of HBM per device.

```python
import jax
import jax.numpy as jnp
from jax import lax

FI = 128
HEADS = 8
HD = 64
TILE = 32
DEG = 8
ROWS_DEV = 256
TILES_DEV = 8
PEERS = 16
NODES = 4096
N_ROW = 16


def request_table(key):
    base = jax.random.fold_in(key, 101)
    first, second = jax.random.split(base)
    valid = jax.random.randint(first, (PEERS, PEERS), 0, 10) < 7
    valid = valid | jnp.eye(PEERS, dtype=bool)
    chosen = jax.random.randint(second, (PEERS, PEERS), 0, TILES_DEV)
    return jnp.where(valid, chosen, -1).astype(jnp.int32)


def draw_requests(key, part):
    table = request_table(key)
    return table


def draw_src_slot(key, part):
    table = request_table(key)
    key = jax.random.fold_in(key, 5)
    first, second = jax.random.split(key)
    valid = (table >= 0).astype(jnp.int32)
    column = jnp.arange(PEERS, dtype=jnp.int32)[None, :]
    order_score = (1 - valid) * PEERS + column
    order = jnp.argsort(order_score, axis=1, stable=True).astype(jnp.int32)
    count = jnp.sum(valid, axis=1)
    node_dev = jnp.arange(NODES, dtype=jnp.int32) // ROWS_DEV
    pick = jax.random.randint(first, (NODES, DEG), 0, 1 << 20) % count[node_dev][:, None]
    peer = jnp.take_along_axis(order[node_dev], pick, axis=1)
    within = jax.random.randint(second, (NODES, DEG), 0, TILE)
    return (peer * TILE + within).astype(jnp.int32)


def draw_edge_mask(key, part):
    key = jax.random.fold_in(key, 9)
    live = (jax.random.randint(key, (NODES, DEG), 0, 10) < 6).astype(jnp.int32)
    return live.at[:, 0].set(1)


def draw_features(key, part):
    key = jax.random.fold_in(key, 7)
    first = jax.random.fold_in(key, 0)
    return jnp.clip(jax.random.normal(first, (NODES, FI), jnp.float32), -6.0, 6.0)


def level_of(key, extent, cuts, least, high):
    def one(axis_at, parts):
        steps = jax.random.uniform(jax.random.fold_in(jax.random.fold_in(key, 6), axis_at), (parts,), jnp.float32, least / len(cuts), high / len(cuts))
        return jnp.repeat(jnp.exp(steps), extent[axis_at] // parts).reshape((-1,) + (1,) * (len(extent) - axis_at - 1))

    level = one(*cuts[0])
    for cut in cuts[1:]:
        level = level * one(*cut)
    return level


def normal_values(rng, dims, spread, limit, cuts=(), kind=jnp.bfloat16):
    values = spread * jax.random.normal(rng, dims, jnp.float32)
    if cuts:
        values = values * level_of(rng, dims, cuts, -0.22, 0.18)
    return jnp.clip(values, -limit, limit).astype(kind)


def setup_inputs(seed: int = 0, part: int = 0) -> dict:
    splits = jax.random.split(jax.random.key(seed), 9)
    part_keys = jax.random.split(jax.random.fold_in(splits[8], part), 9)
    return {
        "features": draw_features(jax.random.fold_in(jax.random.fold_in(splits[8], part), 71), part),
        "w_left": normal_values(splits[1], (FI, HEADS * HD), FI ** -0.5, 0.5, (), jnp.float32),
        "w_right": normal_values(splits[2], (FI, HEADS * HD), FI ** -0.5, 0.5, (), jnp.float32),
        "attention": normal_values(splits[3], (HEADS, HD), HD ** -0.5, 0.75, (), jnp.float32),
        "requests": draw_requests(jax.random.fold_in(jax.random.fold_in(splits[8], part), 71), part),
        "src_slot": draw_src_slot(jax.random.fold_in(jax.random.fold_in(splits[8], part), 71), part),
        "edge_mask": draw_edge_mask(jax.random.fold_in(jax.random.fold_in(splits[8], part), 71), part),
        "g_out": normal_values(part_keys[7], (NODES, HEADS * HD), 1.0, 6.0, ((0, 16),), jnp.float32),
    }


HIGH_PRECISION = lax.Precision.HIGHEST


def attend(left_e, right_rows, attention, live, g_rows):
    z = left_e + right_rows[:, None]
    slope = jnp.where(z > 0, 1.0, 0.2).astype(z.dtype)
    u = z * slope
    score = jnp.einsum("behc,hc->beh", u, attention, precision=HIGH_PRECISION)
    alive = live[:, :, None] > 0
    score = jnp.where(alive, score, -1e30)
    top = jnp.max(score, axis=1, keepdims=True)
    weights = jnp.exp(score - top) * alive.astype(score.dtype)
    prob = weights / jnp.sum(weights, axis=1, keepdims=True)
    out_rows = jnp.einsum("beh,behc->bhc", prob, left_e, precision=HIGH_PRECISION)
    dprob = jnp.einsum("bhc,behc->beh", g_rows, left_e, precision=HIGH_PRECISION)
    dscore = prob * (dprob - jnp.sum(prob * dprob, axis=1, keepdims=True))
    inner = dscore[..., None] * attention[None, None] * slope
    d_left = prob[..., None] * g_rows[:, None] + inner
    right_gradient = jnp.sum(inner, axis=1)
    d_att = jnp.einsum("beh,behc->hc", dscore, u, precision=HIGH_PRECISION)
    return out_rows, d_left, right_gradient, d_att


def reference(features, w_left, w_right, attention, requests, src_slot, edge_mask, g_out):
    width = HEADS * HD
    left = jnp.dot(features, w_left, precision=HIGH_PRECISION, preferred_element_type=jnp.float32)
    right = jnp.dot(features, w_right, precision=HIGH_PRECISION, preferred_element_type=jnp.float32)
    node_dev = jnp.arange(NODES, dtype=jnp.int32) // ROWS_DEV
    peer = (src_slot // TILE).astype(jnp.int32)
    tile_of = requests[node_dev[:, None], peer]
    source = (peer * ROWS_DEV + tile_of * TILE + src_slot % TILE).astype(jnp.int32)

    def step(carry, blocks):
        d_left_all, d_att = carry
        src_b, live_batch_mask, right_b, g_b = blocks
        left_e = left[src_b].reshape(ROWS_DEV, DEG, HEADS, HD)
        out_b, d_l, d_r, d_a = attend(left_e, right_b.reshape(ROWS_DEV, HEADS, HD), attention, live_batch_mask, g_b.reshape(ROWS_DEV, HEADS, HD))
        d_left_all = d_left_all.at[src_b.reshape(-1)].add(d_l.reshape(-1, width))
        return (d_left_all, d_att + d_a), (out_b.reshape(ROWS_DEV, width), d_r.reshape(ROWS_DEV, width))

    blocks = (source.reshape(N_ROW, ROWS_DEV, DEG), edge_mask.reshape(N_ROW, ROWS_DEV, DEG),
              right.reshape(N_ROW, ROWS_DEV, width), g_out.reshape(N_ROW, ROWS_DEV, width))
    start = (jnp.zeros((NODES, width), jnp.float32), jnp.zeros((HEADS, HD), jnp.float32))
    (d_left_all, grad_att), (out_blocks, d_right_blocks) = lax.scan(step, start, blocks)
    out = out_blocks.reshape(NODES, width)
    right_gradient = d_right_blocks.reshape(NODES, width)
    feature_gradient = jnp.dot(d_left_all, w_left.T, precision=HIGH_PRECISION, preferred_element_type=jnp.float32) + jnp.dot(right_gradient, w_right.T, precision=HIGH_PRECISION, preferred_element_type=jnp.float32)
    grad_left = jnp.dot(features.T, d_left_all, precision=HIGH_PRECISION, preferred_element_type=jnp.float32)
    grad_right = jnp.dot(features.T, right_gradient, precision=HIGH_PRECISION, preferred_element_type=jnp.float32)
    return (out, feature_gradient, grad_left, grad_right, grad_att)
```

```python
import functools

import jax
import jax.numpy as jnp
from jax import lax
from jax.experimental import pallas as pl
from jax.experimental.pallas import tpu as pltpu
from jax.sharding import PartitionSpec as P

FI = 128
HEADS = 8
HD = 64
TILE = 32
DEG = 8
WIDTH = HEADS * HD
LANES = 128
CHUNK = 512

HIGHEST = lax.Precision.HIGHEST
MESH = pl.DeviceIdType.MESH
BF16 = jnp.bfloat16
F32 = jnp.float32


def dot(a, b, dims=((1,), (0,)), precision=None):
    return lax.dot_general(a, b, (dims, ((), ())), precision=precision, preferred_element_type=F32)


def split(x):
    hi = x.astype(BF16)
    return hi, (x - hi.astype(F32)).astype(BF16)


def split3(x):
    hi = x.astype(BF16)
    rest = x - hi.astype(F32)
    mid = rest.astype(BF16)
    return hi, mid, (rest - mid.astype(F32)).astype(BF16)


def greet(n, me, barrier):
    @pl.loop(1, n)
    def _(k):
        pl.semaphore_signal(barrier, inc=1, device_id={"row": lax.rem(me + k, n)}, device_id_type=MESH)

    pl.semaphore_wait(barrier, n - 1)


def fetch_kernel(n, req_ref, feat_ref, fetched_ref, asked_ref, ask_out, tile_out, ask_in, tile_in, sems):
    me = lax.axis_index("row")
    tiles = feat_ref.shape[0] // TILE
    barrier = pltpu.get_barrier_semaphore()

    def ask(k):
        peer = lax.rem(me + k, n)
        return pltpu.make_async_remote_copy(
            src_ref=ask_out.at[peer], dst_ref=ask_in.at[me], send_sem=sems.at[0, k], recv_sem=sems.at[1, k],
            device_id={"row": peer}, device_id_type=MESH)

    def give(k):
        peer = lax.rem(me + k, n)
        return pltpu.make_async_remote_copy(
            src_ref=tile_out.at[peer], dst_ref=tile_in.at[me], send_sem=sems.at[2, k], recv_sem=sems.at[3, k],
            device_id={"row": peer}, device_id_type=MESH)

    for p in range(n):
        ask_out[p] = jnp.full((8, LANES), req_ref[0, p], jnp.int32)
    greet(n, me, barrier)

    @pl.loop(1, n)
    def _(k):
        ask(k).start()

    feats = [feat_ref[t * TILE:(t + 1) * TILE].reshape(TILE // 8, 8, FI) for t in range(tiles)]

    def chosen(want):
        total = jnp.zeros((TILE // 8, 8, FI), F32)
        for t in range(tiles):
            total = total + jnp.where((want == t)[None], feats[t], 0.0)
        return total.reshape(TILE, FI)

    tile_in[me] = chosen(ask_out[me])
    ask_in[me] = ask_out[me]

    @pl.loop(1, n)
    def _(j):
        k = n - j
        ask(k).wait_recv()
        peer = lax.rem(me + j, n)
        tile_out[peer] = chosen(ask_in[peer])
        give(j).start()

    @pl.loop(1, n)
    def _(k):
        give(k).wait_recv()
        ask(k).wait_send()
        give(k).wait_send()

    fetched_ref[...] = tile_in[...].reshape(n * TILE, FI)
    asked_ref[...] = ask_in[...]


def local_kernel(n, fetched_ref, feat_ref, wl_ref, wr_ref, att_ref, slot_ref, mask_ref, g_ref,
                 out_ref, ret_ref, fg_ref, msg_ref, hi_ref, mid_ref, lo_ref, le_ref, dhi_ref, dlo_ref, wg_ref):
    rows = feat_ref.shape[0]
    slots_all = fetched_ref.shape[0]
    chunks = slots_all // CHUNK
    left = dot(fetched_ref[...], wl_ref[...], precision=HIGHEST) if chunks == 1 else None
    if chunks == 1:
        hi_ref[...], mid_ref[...], lo_ref[...] = split3(left)
    else:
        @pl.loop(0, chunks)
        def _(c):
            at = pl.ds(pl.multiple_of(c * CHUNK, CHUNK), CHUNK)
            hi_ref[at], mid_ref[at], lo_ref[at] = split3(dot(fetched_ref[at], wl_ref[...], precision=HIGHEST))
    right = dot(feat_ref[...], wr_ref[...], precision=HIGHEST)
    att = att_ref[...]
    g = g_ref[...]
    slot = slot_ref[...]

    row_head = lax.broadcasted_iota(jnp.int32, (WIDTH, LANES), 0) // HD
    col = lax.broadcasted_iota(jnp.int32, (WIDTH, LANES), 1)
    row_match = row_head == (col & 7)
    col_edge = (col >> 3) & 7
    score = jnp.zeros((rows, LANES), F32)
    dp = jnp.zeros((rows, LANES), F32)
    slot_lane = lax.broadcasted_iota(jnp.int32, (rows, CHUNK), 1)
    for e in range(DEG):
        here = slot[:, e:e + 1]
        if chunks == 1:
            pick = (slot_lane == here).astype(F32).astype(BF16)
            left_e = dot(pick, hi_ref[...]) + (dot(pick, mid_ref[...]) + dot(pick, lo_ref[...]))
            le_ref[e] = left_e
        else:
            le_ref[e] = jnp.zeros((rows, WIDTH), F32)

            @pl.loop(0, chunks)
            def _(c):
                at = pl.ds(pl.multiple_of(c * CHUNK, CHUNK), CHUNK)
                pick = (slot_lane + c * CHUNK == here).astype(F32).astype(BF16)
                le_ref[e] += dot(pick, hi_ref[at]) + (dot(pick, mid_ref[at]) + dot(pick, lo_ref[at]))

            left_e = le_ref[e]
        z = left_e + right
        group = (row_match & (col_edge == e)).astype(F32).astype(BF16)
        v_hi, v_lo = split(jnp.maximum(z, 0.2 * z) * att)
        score = score + (dot(v_hi, group) + dot(v_lo, group))
        p_hi, p_lo = split(g * left_e)
        dp = dp + (dot(p_hi, group) + dot(p_lo, group))

    spread = (lax.broadcasted_iota(jnp.int32, (DEG, LANES), 0)
              == ((lax.broadcasted_iota(jnp.int32, (DEG, LANES), 1) >> 3) & 7)).astype(F32)
    alive = dot((mask_ref[...] > 0).astype(F32), spread) > 0.5

    def over_edges(x, op):
        for shift in (8, 16, 32):
            x = op(x, pltpu.roll(x, shift, 1))
        return x

    score = jnp.where(alive, score, -1e30)
    top = over_edges(score, jnp.maximum)
    weights = jnp.where(alive, jnp.exp(score - top), 0.0)
    prob = weights / over_edges(weights, jnp.add)
    ds = prob * (dp - over_edges(prob * dp, jnp.add))
    first_half = lax.broadcasted_iota(jnp.int32, (rows, LANES), 1) < LANES // 2

    def halves(x):
        hi = x.astype(BF16).astype(F32)
        return jnp.where(first_half, hi, x - hi).astype(BF16)

    prob_hl = halves(prob)
    ds_hl = halves(ds)

    krow = lax.broadcasted_iota(jnp.int32, (LANES, WIDTH), 0)
    kmatch = (krow & 7) == lax.broadcasted_iota(jnp.int32, (LANES, WIDTH), 1) // HD
    kedge = (krow >> 3) & 7
    out = jnp.zeros((rows, WIDTH), F32)
    d_right = jnp.zeros((rows, WIDTH), F32)
    d_att = jnp.zeros((8, WIDTH), F32)
    for e in range(DEG):
        widen = (kmatch & (kedge == e)).astype(F32).astype(BF16)
        prob_w = dot(prob_hl, widen)
        ds_w = dot(ds_hl, widen)
        left_e = le_ref[e]
        z = left_e + right
        slope = jnp.where(z > 0, 1.0, 0.2)
        out = out + prob_w * left_e
        t = ds_w * slope
        inner = t * att
        d_right = d_right + inner
        d_att = d_att + jnp.sum((t * z).reshape(rows // 8, 8, WIDTH), axis=0)
        dhi_ref[e * rows:(e + 1) * rows], dlo_ref[e * rows:(e + 1) * rows] = split(prob_w * g + inner)
    out_ref[...] = out

    slot_t = slot.T
    slot_row = lax.broadcasted_iota(jnp.int32, (CHUNK, rows), 0)

    def scatter(c):
        total = jnp.zeros((CHUNK, WIDTH), F32)
        for e in range(DEG):
            put = (slot_row + c * CHUNK == slot_t[e:e + 1]).astype(F32).astype(BF16)
            total = total + (dot(put, dhi_ref[e * rows:(e + 1) * rows]) + dot(put, dlo_ref[e * rows:(e + 1) * rows]))
        return total

    if chunks == 1:
        d_left = scatter(0)
        ret_ref[...] = dot(d_left, wl_ref[...], ((1,), (1,)), precision=HIGHEST)
        wg_ref[0:FI] = dot(fetched_ref[...].T, d_left, precision=HIGHEST)
    else:
        wg_ref[0:FI] = jnp.zeros((FI, WIDTH), F32)

        @pl.loop(0, chunks)
        def _(c):
            at = pl.ds(pl.multiple_of(c * CHUNK, CHUNK), CHUNK)
            d_left = scatter(c)
            ret_ref[at] = dot(d_left, wl_ref[...], ((1,), (1,)), precision=HIGHEST)
            wg_ref[0:FI] += dot(fetched_ref[at].T, d_left, precision=HIGHEST)
    fg_ref[...] = dot(d_right, wr_ref[...], ((1,), (1,)), precision=HIGHEST)
    wg_ref[FI:2 * FI] = dot(feat_ref[...].T, d_right, precision=HIGHEST)

    unit, per = units(n)
    for u in range(n * per):
        rb, lb = u // 4, u % 4
        msg_ref[u // per, (u % per) * unit:(u % per + 1) * unit] = (
            wg_ref[rb * unit:(rb + 1) * unit, lb * LANES:(lb + 1) * LANES])
    att_row = jnp.sum(d_att, axis=0, keepdims=True)
    tail = jnp.concatenate([att_row[:, b * LANES:(b + 1) * LANES] for b in range(4)] + [jnp.zeros((4, LANES), F32)], axis=0)
    for p in range(n):
        msg_ref[p, per * unit:] = tail


def units(n):
    unit = max(8, 2 * FI // n)
    return unit, (2 * FI // unit) * 4 // n


def return_kernel(n, ret_ref, fg_ref, msg_ref, asked_ref, fgo_ref, gl_ref, gr_ref, ga_ref,
                  ret_in, msg_in, sum_out, sum_in, sems):
    me = lax.axis_index("row")
    unit, per = units(n)
    body = unit * per
    barrier = pltpu.get_barrier_semaphore()

    def remote(src, dst, lane, k):
        return pltpu.make_async_remote_copy(
            src_ref=src, dst_ref=dst, send_sem=sems.at[2 * lane, k], recv_sem=sems.at[2 * lane + 1, k],
            device_id={"row": lax.rem(me + k, n)}, device_id_type=MESH)

    def send_msg(k):
        return remote(msg_ref.at[lax.rem(me + k, n)], msg_in.at[me], 0, k)

    def send_ret(k):
        return remote(ret_ref.at[lax.rem(me + k, n)], ret_in.at[me], 1, k)

    def send_sum(k):
        return remote(sum_out, sum_in.at[me], 2, k)

    greet(n, me, barrier)

    @pl.loop(1, n)
    def _(k):
        send_msg(k).start()

    @pl.loop(1, n)
    def _(k):
        send_ret(k).start()

    msg_in[me] = msg_ref[me]
    ret_in[me] = ret_ref[me]

    @pl.loop(1, n)
    def _(k):
        send_msg(k).wait_recv()

    total = lax.fori_loop(1, n, lambda p, acc: acc + msg_in[p], msg_in[0])
    sum_out[...] = total[:body]

    @pl.loop(1, n)
    def _(k):
        send_sum(k).start()

    sum_in[me] = total[:body]
    for b in range(4):
        ga_ref[2 * b:2 * b + 1] = total[body + b:body + b + 1, :HD]
        ga_ref[2 * b + 1:2 * b + 2] = total[body + b:body + b + 1, HD:]

    @pl.loop(1, n)
    def _(k):
        send_ret(k).wait_recv()

    tiles = fg_ref.shape[0] // TILE

    def collect(q, acc):
        want = asked_ref[q]
        back = ret_in[q].reshape(TILE // 8, 8, FI)
        return tuple(acc[t] + jnp.where((want == t)[None], back, 0.0) for t in range(tiles))

    start = tuple(fg_ref[t * TILE:(t + 1) * TILE].reshape(TILE // 8, 8, FI) for t in range(tiles))
    done = lax.fori_loop(0, n, collect, start)
    for t in range(tiles):
        fgo_ref[t * TILE:(t + 1) * TILE] = done[t].reshape(TILE, FI)

    @pl.loop(1, n)
    def _(k):
        send_sum(k).wait_recv()

    for u in range(n * per):
        rb, lb = u // 4, u % 4
        ref, base = (gl_ref, 0) if rb * unit < FI else (gr_ref, FI)
        ref[rb * unit - base:(rb + 1) * unit - base, lb * LANES:(lb + 1) * LANES] = (
            sum_in[u // per, (u % per) * unit:(u % per + 1) * unit])

    @pl.loop(1, n)
    def _(k):
        send_msg(k).wait_send()
        send_ret(k).wait_send()
        send_sum(k).wait_send()


def on_device(features, w_left, w_right, attention, requests, src_slot, edge_mask, g_out):
    n = lax.axis_size("row")
    rows = features.shape[0]
    vmem = pl.BlockSpec(memory_space=pltpu.VMEM)
    smem = pl.BlockSpec(memory_space=pltpu.SMEM)
    limit = 56 * 2**20 if n > 16 else 40 * 2**20

    def shape(*dims, kind=F32):
        return jax.ShapeDtypeStruct(dims, kind)

    fetched, asked = pl.pallas_call(
        functools.partial(fetch_kernel, n),
        out_shape=(shape(n * TILE, FI), shape(n, 8, LANES, kind=jnp.int32)),
        in_specs=[smem, vmem],
        out_specs=(vmem, vmem),
        scratch_shapes=[
            pltpu.VMEM((n, 8, LANES), jnp.int32),
            pltpu.VMEM((n, TILE, FI), F32),
            pltpu.VMEM((n, 8, LANES), jnp.int32),
            pltpu.VMEM((n, TILE, FI), F32),
            pltpu.SemaphoreType.DMA((4, n)),
        ],
        compiler_params=pltpu.CompilerParams(collective_id=0, has_side_effects=True, vmem_limit_bytes=limit),
        name="fetch",
    )(requests, features)

    unit, per = units(n)
    body = unit * per
    out, ret, fg, msg = pl.pallas_call(
        functools.partial(local_kernel, n),
        out_shape=(shape(rows, WIDTH), shape(n * TILE, FI), shape(rows, FI), shape(n, body + 8, LANES)),
        in_specs=[vmem] * 8,
        out_specs=(vmem,) * 4,
        scratch_shapes=[
            pltpu.VMEM((n * TILE, WIDTH), BF16),
            pltpu.VMEM((n * TILE, WIDTH), BF16),
            pltpu.VMEM((n * TILE, WIDTH), BF16),
            pltpu.VMEM((DEG, rows, WIDTH), F32),
            pltpu.VMEM((DEG * rows, WIDTH), BF16),
            pltpu.VMEM((DEG * rows, WIDTH), BF16),
            pltpu.VMEM((2 * FI, WIDTH), F32),
        ],
        compiler_params=pltpu.CompilerParams(vmem_limit_bytes=limit),
        name="local",
    )(fetched, features, w_left, w_right, attention.reshape(1, WIDTH), src_slot, edge_mask, g_out)

    feature_gradient, grad_left, grad_right, grad_att = pl.pallas_call(
        functools.partial(return_kernel, n),
        out_shape=(shape(rows, FI), shape(FI, WIDTH), shape(FI, WIDTH), shape(HEADS, HD)),
        in_specs=[vmem] * 4,
        out_specs=(vmem,) * 4,
        scratch_shapes=[
            pltpu.VMEM((n, TILE, FI), F32),
            pltpu.VMEM((n, body + 8, LANES), F32),
            pltpu.VMEM((body, LANES), F32),
            pltpu.VMEM((n, body, LANES), F32),
            pltpu.SemaphoreType.DMA((6, n)),
        ],
        compiler_params=pltpu.CompilerParams(collective_id=1, has_side_effects=True, vmem_limit_bytes=limit),
        name="give_back",
    )(ret.reshape(n, TILE, FI), fg, msg, asked)
    return (out, feature_gradient, grad_left, grad_right, grad_att)


def solution(mesh):
    rowwise = P(("group", "row"), None)
    in_specs = (rowwise, P(), P(), P(), rowwise, rowwise, rowwise, rowwise)
    out_specs = (rowwise, rowwise, P("group", None), P("group", None), P("group", None))
    return jax.shard_map(
        on_device, mesh=mesh, in_specs=in_specs, out_specs=out_specs, check_vma=False
    )
```

```python
import functools

import jax
import jax.numpy as jnp
from jax import lax
from jax.experimental import pallas as pl
from jax.experimental.pallas import tpu as pltpu
from jax.sharding import PartitionSpec as P

FI = 128
HEADS = 8
HD = 64
TILE = 32
DEG = 8
WIDTH = HEADS * HD
LANES = 128
CHUNK = 512

HIGHEST = lax.Precision.HIGHEST
MESH = pl.DeviceIdType.MESH
BF16 = jnp.bfloat16
F32 = jnp.float32


def dot(a, b, dims=((1,), (0,)), precision=None):
    return lax.dot_general(a, b, (dims, ((), ())), precision=precision, preferred_element_type=F32)


def split(x):
    hi = x.astype(BF16)
    return hi, (x - hi.astype(F32)).astype(BF16)


def split3(x):
    hi = x.astype(BF16)
    rest = x - hi.astype(F32)
    mid = rest.astype(BF16)
    return hi, mid, (rest - mid.astype(F32)).astype(BF16)


def greet(n, me, barrier):
    @pl.loop(1, n)
    def _(k):
        pl.semaphore_signal(barrier, inc=1, device_id={"row": lax.rem(me + k, n)}, device_id_type=MESH)

    pl.semaphore_wait(barrier, n - 1)


def fetch_kernel(n, req_ref, feat_ref, fetched_ref, asked_ref, ask_out, tile_out, ask_in, tile_in, sems):
    me = lax.axis_index("row")
    tiles = feat_ref.shape[0] // TILE
    barrier = pltpu.get_barrier_semaphore()

    def ask(k):
        peer = lax.rem(me + k, n)
        return pltpu.make_async_remote_copy(
            src_ref=ask_out.at[peer], dst_ref=ask_in.at[me], send_sem=sems.at[0, k], recv_sem=sems.at[1, k],
            device_id={"row": peer}, device_id_type=MESH)

    def give(k):
        peer = lax.rem(me + k, n)
        return pltpu.make_async_remote_copy(
            src_ref=tile_out.at[peer], dst_ref=tile_in.at[me], send_sem=sems.at[2, k], recv_sem=sems.at[3, k],
            device_id={"row": peer}, device_id_type=MESH)

    for p in range(n):
        ask_out[p] = jnp.full((8, LANES), req_ref[0, p], jnp.int32)
    greet(n, me, barrier)

    @pl.loop(1, n)
    def _(k):
        ask(k).start()

    feats = [feat_ref[t * TILE:(t + 1) * TILE].reshape(TILE // 8, 8, FI) for t in range(tiles)]

    def chosen(want):
        total = jnp.zeros((TILE // 8, 8, FI), F32)
        for t in range(tiles):
            total = total + jnp.where((want == t)[None], feats[t], 0.0)
        return total.reshape(TILE, FI)

    tile_in[me] = chosen(ask_out[me])
    ask_in[me] = ask_out[me]

    @pl.loop(1, n)
    def _(j):
        k = n - j
        ask(k).wait_recv()
        peer = lax.rem(me + j, n)
        tile_out[peer] = chosen(ask_in[peer])
        give(j).start()

    @pl.loop(1, n)
    def _(k):
        give(k).wait_recv()
        ask(k).wait_send()
        give(k).wait_send()

    fetched_ref[...] = tile_in[...].reshape(n * TILE, FI)
    asked_ref[...] = ask_in[...]


def local_kernel(n, fetched_ref, feat_ref, wl_ref, wr_ref, att_ref, slot_ref, mask_ref, g_ref,
                 out_ref, ret_ref, fg_ref, msg_ref, tail_ref, hi_ref, mid_ref, lo_ref, le_ref, dhi_ref, dlo_ref, wg_ref):
    rows = feat_ref.shape[0]
    slots_all = fetched_ref.shape[0]
    chunks = slots_all // CHUNK
    left = dot(fetched_ref[...], wl_ref[...], precision=HIGHEST) if chunks == 1 else None
    if chunks == 1:
        hi_ref[...], mid_ref[...], lo_ref[...] = split3(left)
    else:
        @pl.loop(0, chunks)
        def _(c):
            at = pl.ds(pl.multiple_of(c * CHUNK, CHUNK), CHUNK)
            hi_ref[at], mid_ref[at], lo_ref[at] = split3(dot(fetched_ref[at], wl_ref[...], precision=HIGHEST))
    right = dot(feat_ref[...], wr_ref[...], precision=HIGHEST)
    att = jnp.concatenate([att_ref[h:h + 1, :] for h in range(HEADS)], axis=1)
    g = g_ref[...]
    slot_t = slot_ref[...]
    slot = slot_t.T

    row_head = lax.broadcasted_iota(jnp.int32, (WIDTH, LANES), 0) // HD
    col = lax.broadcasted_iota(jnp.int32, (WIDTH, LANES), 1)
    row_match = row_head == (col & 7)
    col_edge = (col >> 3) & 7
    score = jnp.zeros((rows, LANES), F32)
    dp = jnp.zeros((rows, LANES), F32)
    slot_lane = lax.broadcasted_iota(jnp.int32, (rows, CHUNK), 1)
    for e in range(DEG):
        here = slot[:, e:e + 1]
        if chunks == 1:
            pick = (slot_lane == here).astype(F32).astype(BF16)
            left_e = dot(pick, hi_ref[...]) + (dot(pick, mid_ref[...]) + dot(pick, lo_ref[...]))
            le_ref[e] = left_e
        else:
            le_ref[e] = jnp.zeros((rows, WIDTH), F32)

            @pl.loop(0, chunks)
            def _(c):
                at = pl.ds(pl.multiple_of(c * CHUNK, CHUNK), CHUNK)
                pick = (slot_lane + c * CHUNK == here).astype(F32).astype(BF16)
                le_ref[e] += dot(pick, hi_ref[at]) + (dot(pick, mid_ref[at]) + dot(pick, lo_ref[at]))

            left_e = le_ref[e]
        z = left_e + right
        group = (row_match & (col_edge == e)).astype(F32).astype(BF16)
        v_hi, v_lo = split(jnp.maximum(z, 0.2 * z) * att)
        score = score + (dot(v_hi, group) + dot(v_lo, group))
        p_hi, p_lo = split(g * left_e)
        dp = dp + (dot(p_hi, group) + dot(p_lo, group))

    spread = (lax.broadcasted_iota(jnp.int32, (DEG, LANES), 0)
              == ((lax.broadcasted_iota(jnp.int32, (DEG, LANES), 1) >> 3) & 7)).astype(F32)
    alive = dot((mask_ref[...].T > 0).astype(F32), spread) > 0.5

    def over_edges(x, op):
        for shift in (8, 16, 32):
            x = op(x, pltpu.roll(x, shift, 1))
        return x

    score = jnp.where(alive, score, -1e30)
    top = over_edges(score, jnp.maximum)
    weights = jnp.where(alive, jnp.exp(score - top), 0.0)
    prob = weights / over_edges(weights, jnp.add)
    ds = prob * (dp - over_edges(prob * dp, jnp.add))
    first_half = lax.broadcasted_iota(jnp.int32, (rows, LANES), 1) < LANES // 2

    def halves(x):
        hi = x.astype(BF16).astype(F32)
        return jnp.where(first_half, hi, x - hi).astype(BF16)

    prob_hl = halves(prob)
    ds_hl = halves(ds)

    krow = lax.broadcasted_iota(jnp.int32, (LANES, WIDTH), 0)
    kmatch = (krow & 7) == lax.broadcasted_iota(jnp.int32, (LANES, WIDTH), 1) // HD
    kedge = (krow >> 3) & 7
    out = jnp.zeros((rows, WIDTH), F32)
    d_right = jnp.zeros((rows, WIDTH), F32)
    d_att = jnp.zeros((8, WIDTH), F32)
    for e in range(DEG):
        widen = (kmatch & (kedge == e)).astype(F32).astype(BF16)
        prob_w = dot(prob_hl, widen)
        ds_w = dot(ds_hl, widen)
        left_e = le_ref[e]
        z = left_e + right
        slope = jnp.where(z > 0, 1.0, 0.2)
        out = out + prob_w * left_e
        t = ds_w * slope
        inner = t * att
        d_right = d_right + inner
        d_att = d_att + jnp.sum((t * z).reshape(rows // 8, 8, WIDTH), axis=0)
        dhi_ref[e * rows:(e + 1) * rows], dlo_ref[e * rows:(e + 1) * rows] = split(prob_w * g + inner)
    out_ref[...] = out

    slot_row = lax.broadcasted_iota(jnp.int32, (CHUNK, rows), 0)

    def scatter(c):
        total = jnp.zeros((CHUNK, WIDTH), F32)
        for e in range(DEG):
            put = (slot_row + c * CHUNK == slot_t[e:e + 1]).astype(F32).astype(BF16)
            total = total + (dot(put, dhi_ref[e * rows:(e + 1) * rows]) + dot(put, dlo_ref[e * rows:(e + 1) * rows]))
        return total

    if chunks == 1:
        d_left = scatter(0)
        ret_ref[...] = dot(d_left, wl_ref[...], ((1,), (1,)), precision=HIGHEST)
        wg_ref[0:FI] = dot(fetched_ref[...].T, d_left, precision=HIGHEST)
    else:
        wg_ref[0:FI] = jnp.zeros((FI, WIDTH), F32)

        @pl.loop(0, chunks)
        def _(c):
            at = pl.ds(pl.multiple_of(c * CHUNK, CHUNK), CHUNK)
            d_left = scatter(c)
            ret_ref[at] = dot(d_left, wl_ref[...], ((1,), (1,)), precision=HIGHEST)
            wg_ref[0:FI] += dot(fetched_ref[at].T, d_left, precision=HIGHEST)
    fg_ref[...] = dot(d_right, wr_ref[...], ((1,), (1,)), precision=HIGHEST)
    wg_ref[FI:2 * FI] = dot(feat_ref[...].T, d_right, precision=HIGHEST)

    unit, per = units(n)
    for u in range(n * per):
        rb, lb = u // 4, u % 4
        msg_ref[u // per, (u % per) * unit:(u % per + 1) * unit] = (
            wg_ref[rb * unit:(rb + 1) * unit, lb * LANES:(lb + 1) * LANES])
    att_row = jnp.sum(d_att, axis=0, keepdims=True)
    tail = jnp.concatenate([att_row[:, b * LANES:(b + 1) * LANES] for b in range(4)] + [jnp.zeros((4, LANES), F32)], axis=0)
    tail_ref[...] = tail


def units(n):
    unit = max(8, 2 * FI // n)
    return unit, (2 * FI // unit) * 4 // n


def levels(n):
    mid = 1
    while mid * mid * 4 <= n // 2:
        mid *= 2
    return n // 2 // mid, mid


def return_kernel(n, ret_ref, fg_ref, msg_ref, att_ref, asked_ref, fgo_ref, gl_ref, gr_ref, ga_ref,
                  ret_in, half_in, half, mid_in, part, outer_in, gathered, att_core, att_mid, att_outer,
                  ret_sems, sems, att_sems):
    me = lax.axis_index("row")
    outer, mid = levels(n)
    plane = mid * outer
    o, m, c = me // (2 * mid), lax.rem(me // 2, mid), lax.rem(me, 2)
    unit, per = units(n)
    barrier = pltpu.get_barrier_semaphore()

    def remote(src, dst, peer, sem, slot):
        return pltpu.make_async_remote_copy(
            src_ref=src, dst_ref=dst, send_sem=sem.at[0, slot], recv_sem=sem.at[1, slot],
            device_id={"row": peer}, device_id_type=MESH)

    def send_ret(k):
        peer = lax.rem(me + k, n)
        return remote(ret_ref.at[peer], ret_in.at[me], peer, ret_sems, k)

    def mid_peer(k):
        at = lax.rem(m + k, mid)
        return at, (o * mid + at) * 2 + c

    def outer_peer(k):
        at = lax.rem(o + k, outer)
        return at, (at * mid + m) * 2 + c

    partner = me + 1 - 2 * c
    first, second, third, fourth = 1, mid, mid + outer, mid + 2 * outer
    mine = pl.ds(c * plane, plane)
    block = pl.ds(c * plane + m * outer, outer)
    spot = c * plane + m * outer + o

    greet(n, me, barrier)

    to_core = [
        remote(att_ref, att_core, partner, att_sems, 0),
        remote(msg_ref.at[pl.ds((1 - c) * plane, plane)], half_in, partner, sems, 0),
    ]
    for copy in to_core:
        copy.start()

    @pl.loop(1, n)
    def _(k):
        send_ret(k).start()

    ret_in[me] = ret_ref[me]
    for copy in to_core:
        copy.wait_recv()
    att_mid[m] = att_ref[...] + att_core[...]
    half[...] = msg_ref[mine] + half_in[...]

    to_mid = []
    for k in range(1, mid):
        at, peer = mid_peer(k)
        to_mid.append(remote(att_mid.at[m], att_mid.at[m], peer, att_sems, first + k - 1))
        to_mid.append(remote(half.at[pl.ds(at * outer, outer)], mid_in.at[m], peer, sems, first + k - 1))
    for copy in to_mid:
        copy.start()
    for copy in to_mid:
        copy.wait_recv()
    total = half[pl.ds(m * outer, outer)]
    for k in range(1, mid):
        total = total + mid_in[lax.rem(m + k, mid)]
    part[...] = total
    att = att_mid[0]
    for k in range(1, mid):
        att = att + att_mid[k]
    att_outer[o] = att

    to_outer = []
    for k in range(1, outer):
        at, peer = outer_peer(k)
        to_outer.append(remote(att_outer.at[o], att_outer.at[o], peer, att_sems, second + k - 1))
        to_outer.append(remote(part.at[at], outer_in.at[o], peer, sems, second + k - 1))
    for copy in to_outer:
        copy.start()
    for copy in to_outer:
        copy.wait_recv()
    total = part[o]
    for k in range(1, outer):
        total = total + outer_in[lax.rem(o + k, outer)]
    gathered[spot] = total

    back_outer = [remote(gathered.at[spot], gathered.at[spot], outer_peer(k)[1], sems, third + k - 1)
                  for k in range(1, outer)]
    for copy in back_outer:
        copy.start()
    att = att_outer[0]
    for k in range(1, outer):
        att = att + att_outer[k]
    for b in range(4):
        ga_ref[2 * b:2 * b + 1] = att[b:b + 1, :HD]
        ga_ref[2 * b + 1:2 * b + 2] = att[b:b + 1, HD:]
    for copy in back_outer:
        copy.wait_recv()

    back_mid = [remote(gathered.at[block], gathered.at[block], mid_peer(k)[1], sems, fourth + k - 1)
                for k in range(1, mid)]
    for copy in back_mid:
        copy.start()

    @pl.loop(1, n)
    def _(k):
        send_ret(k).wait_recv()

    tiles = fg_ref.shape[0] // TILE

    def collect(q, acc):
        want = asked_ref[q]
        back = ret_in[q].reshape(TILE // 8, 8, FI)
        return tuple(acc[t] + jnp.where((want == t)[None], back, 0.0) for t in range(tiles))

    start = tuple(fg_ref[t * TILE:(t + 1) * TILE].reshape(TILE // 8, 8, FI) for t in range(tiles))
    done = lax.fori_loop(0, n, collect, start)
    for t in range(tiles):
        fgo_ref[t * TILE:(t + 1) * TILE] = done[t].reshape(TILE, FI)

    for copy in back_mid:
        copy.wait_recv()
    back_core = remote(gathered.at[mine], gathered.at[mine], partner, sems, fourth + mid - 1)
    back_core.start()
    back_core.wait_recv()

    for u in range(n * per):
        rb, lb = u // 4, u % 4
        ref, base = (gl_ref, 0) if rb * unit < FI else (gr_ref, FI)
        ref[rb * unit - base:(rb + 1) * unit - base, lb * LANES:(lb + 1) * LANES] = (
            gathered[u // per, (u % per) * unit:(u % per + 1) * unit])

    for copy in to_core + to_mid + to_outer + back_outer + back_mid + [back_core]:
        copy.wait_send()

    @pl.loop(1, n)
    def _(k):
        send_ret(k).wait_send()


def on_device(features, w_left, w_right, attention, requests, src_slot, edge_mask, g_out):
    n = lax.axis_size("row")
    rows = features.shape[0]
    vmem = pl.BlockSpec(memory_space=pltpu.VMEM)
    smem = pl.BlockSpec(memory_space=pltpu.SMEM)
    limit = 56 * 2**20 if n > 16 else 40 * 2**20

    def shape(*dims, kind=F32):
        return jax.ShapeDtypeStruct(dims, kind)

    fetched, asked = pl.pallas_call(
        functools.partial(fetch_kernel, n),
        out_shape=(shape(n * TILE, FI), shape(n, 8, LANES, kind=jnp.int32)),
        in_specs=[smem, vmem],
        out_specs=(vmem, vmem),
        scratch_shapes=[
            pltpu.VMEM((n, 8, LANES), jnp.int32),
            pltpu.VMEM((n, TILE, FI), F32),
            pltpu.VMEM((n, 8, LANES), jnp.int32),
            pltpu.VMEM((n, TILE, FI), F32),
            pltpu.SemaphoreType.DMA((4, n)),
        ],
        compiler_params=pltpu.CompilerParams(collective_id=0, has_side_effects=True, vmem_limit_bytes=limit),
        name="fetch",
    )(requests, features)

    unit, per = units(n)
    body = unit * per
    outer, mid = levels(n)
    out, ret, fg, msg, tail = pl.pallas_call(
        functools.partial(local_kernel, n),
        out_shape=(shape(rows, WIDTH), shape(n * TILE, FI), shape(rows, FI), shape(n, body, LANES), shape(8, LANES)),
        in_specs=[vmem] * 8,
        out_specs=(vmem,) * 5,
        scratch_shapes=[
            pltpu.VMEM((n * TILE, WIDTH), BF16),
            pltpu.VMEM((n * TILE, WIDTH), BF16),
            pltpu.VMEM((n * TILE, WIDTH), BF16),
            pltpu.VMEM((DEG, rows, WIDTH), F32),
            pltpu.VMEM((DEG * rows, WIDTH), BF16),
            pltpu.VMEM((DEG * rows, WIDTH), BF16),
            pltpu.VMEM((2 * FI, WIDTH), F32),
        ],
        compiler_params=pltpu.CompilerParams(vmem_limit_bytes=limit),
        name="local",
    )(fetched, features, w_left, w_right, attention, src_slot.T, edge_mask.T, g_out)

    feature_gradient, grad_left, grad_right, grad_att = pl.pallas_call(
        functools.partial(return_kernel, n),
        out_shape=(shape(rows, FI), shape(FI, WIDTH), shape(FI, WIDTH), shape(HEADS, HD)),
        in_specs=[vmem] * 5,
        out_specs=(vmem,) * 4,
        scratch_shapes=[
            pltpu.VMEM((n, TILE, FI), F32),
            pltpu.VMEM((outer * mid, body, LANES), F32),
            pltpu.VMEM((outer * mid, body, LANES), F32),
            pltpu.VMEM((mid, outer, body, LANES), F32),
            pltpu.VMEM((outer, body, LANES), F32),
            pltpu.VMEM((outer, body, LANES), F32),
            pltpu.VMEM((n, body, LANES), F32),
            pltpu.VMEM((8, LANES), F32),
            pltpu.VMEM((mid, 8, LANES), F32),
            pltpu.VMEM((outer, 8, LANES), F32),
            pltpu.SemaphoreType.DMA((2, n)),
            pltpu.SemaphoreType.DMA((2, 2 * (outer + mid))),
            pltpu.SemaphoreType.DMA((2, outer + mid)),
        ],
        compiler_params=pltpu.CompilerParams(collective_id=1, has_side_effects=True, vmem_limit_bytes=limit),
        name="give_back",
    )(ret.reshape(n, TILE, FI), fg, msg, tail, asked)
    return (out, feature_gradient, grad_left, grad_right, grad_att)


def solution(mesh):
    rowwise = P(("group", "row"), None)
    in_specs = (rowwise, P(), P(), P(), rowwise, rowwise, rowwise, rowwise)
    out_specs = (rowwise, rowwise, P("group", None), P("group", None), P("group", None))
    return jax.shard_map(
        on_device, mesh=mesh, in_specs=in_specs, out_specs=out_specs, check_vma=False
    )
```

```python
import functools

import jax
import jax.numpy as jnp
from jax import lax
from jax.experimental import pallas as pl
from jax.experimental.pallas import tpu as pltpu
from jax.sharding import PartitionSpec as P

FI = 128
HEADS = 8
HD = 64
TILE = 32
DEG = 8
WIDTH = HEADS * HD
LANES = 128
CHUNK = 512

HIGHEST = lax.Precision.HIGHEST
MESH = pl.DeviceIdType.MESH
BF16 = jnp.bfloat16
F32 = jnp.float32


def dot(a, b, dims=((1,), (0,)), precision=None):
    return lax.dot_general(a, b, (dims, ((), ())), precision=precision, preferred_element_type=F32)


def split(x):
    hi = x.astype(BF16)
    return hi, (x - hi.astype(F32)).astype(BF16)


def split3(x):
    hi = x.astype(BF16)
    rest = x - hi.astype(F32)
    mid = rest.astype(BF16)
    return hi, mid, (rest - mid.astype(F32)).astype(BF16)


def dot3(a, b, dims=((1,), (0,))):
    a_hi, a_lo = split(a)
    b_hi, b_lo = split(b)
    return dot(a_hi, b_hi, dims) + (dot(a_hi, b_lo, dims) + dot(a_lo, b_hi, dims))


def greet(n, me, barrier):
    @pl.loop(1, n)
    def _(k):
        pl.semaphore_signal(barrier, inc=1, device_id={"row": lax.rem(me + k, n)}, device_id_type=MESH)

    pl.semaphore_wait(barrier, n - 1)


def fetch_kernel(n, req_ref, feat_ref, fetched_ref, asked_ref, ask_out, tile_out, ask_in, tile_in, sems):
    me = lax.axis_index("row")
    tiles = feat_ref.shape[0] // TILE
    barrier = pltpu.get_barrier_semaphore()

    def ask(k):
        peer = lax.rem(me + k, n)
        return pltpu.make_async_remote_copy(
            src_ref=ask_out.at[peer], dst_ref=ask_in.at[me], send_sem=sems.at[0, k], recv_sem=sems.at[1, k],
            device_id={"row": peer}, device_id_type=MESH)

    def give(k):
        peer = lax.rem(me + k, n)
        return pltpu.make_async_remote_copy(
            src_ref=tile_out.at[peer], dst_ref=tile_in.at[me], send_sem=sems.at[2, k], recv_sem=sems.at[3, k],
            device_id={"row": peer}, device_id_type=MESH)

    for p in range(n):
        ask_out[p] = jnp.full((8, LANES), req_ref[0, p], jnp.int32)
    greet(n, me, barrier)

    @pl.loop(1, n)
    def _(k):
        ask(k).start()

    feats = [feat_ref[t * TILE:(t + 1) * TILE].reshape(TILE // 8, 8, FI) for t in range(tiles)]

    def chosen(want):
        total = jnp.zeros((TILE // 8, 8, FI), F32)
        for t in range(tiles):
            total = total + jnp.where((want == t)[None], feats[t], 0.0)
        return total.reshape(TILE, FI)

    tile_in[me] = chosen(ask_out[me])
    ask_in[me] = ask_out[me]

    @pl.loop(1, n)
    def _(j):
        k = n - j
        ask(k).wait_recv()
        peer = lax.rem(me + j, n)
        tile_out[peer] = chosen(ask_in[peer])
        give(j).start()

    @pl.loop(1, n)
    def _(k):
        give(k).wait_recv()
        ask(k).wait_send()
        give(k).wait_send()

    fetched_ref[...] = tile_in[...].reshape(n * TILE, FI)
    asked_ref[...] = ask_in[...]


def local_kernel(n, fetched_ref, feat_ref, wl_ref, wr_ref, att_ref, slot_ref, mask_ref, g_ref,
                 out_ref, ret_ref, fg_ref, msg_ref, tail_ref, hi_ref, mid_ref, lo_ref, le_ref, dhi_ref, dlo_ref, wg_ref):
    rows = feat_ref.shape[0]
    slots_all = fetched_ref.shape[0]
    chunks = slots_all // CHUNK
    left = dot(fetched_ref[...], wl_ref[...], precision=HIGHEST) if chunks == 1 else None
    if chunks == 1:
        hi_ref[...], mid_ref[...], lo_ref[...] = split3(left)
    else:
        @pl.loop(0, chunks)
        def _(c):
            at = pl.ds(pl.multiple_of(c * CHUNK, CHUNK), CHUNK)
            hi_ref[at], mid_ref[at], lo_ref[at] = split3(dot(fetched_ref[at], wl_ref[...], precision=HIGHEST))
    right = dot(feat_ref[...], wr_ref[...], precision=HIGHEST)
    att = jnp.concatenate([att_ref[h:h + 1, :] for h in range(HEADS)], axis=1)
    g = g_ref[...]
    slot_t = slot_ref[...]
    slot = slot_t.T

    row_head = lax.broadcasted_iota(jnp.int32, (WIDTH, LANES), 0) // HD
    col = lax.broadcasted_iota(jnp.int32, (WIDTH, LANES), 1)
    row_match = row_head == (col & 7)
    col_edge = (col >> 3) & 7
    score = jnp.zeros((rows, LANES), F32)
    dp = jnp.zeros((rows, LANES), F32)
    slot_lane = lax.broadcasted_iota(jnp.int32, (rows, CHUNK), 1)
    for e in range(DEG):
        here = slot[:, e:e + 1]
        if chunks == 1:
            pick = (slot_lane == here).astype(F32).astype(BF16)
            left_e = dot(pick, hi_ref[...]) + (dot(pick, mid_ref[...]) + dot(pick, lo_ref[...]))
            le_ref[e] = left_e
        else:
            le_ref[e] = jnp.zeros((rows, WIDTH), F32)

            @pl.loop(0, chunks)
            def _(c):
                at = pl.ds(pl.multiple_of(c * CHUNK, CHUNK), CHUNK)
                pick = (slot_lane + c * CHUNK == here).astype(F32).astype(BF16)
                le_ref[e] += dot(pick, hi_ref[at]) + (dot(pick, mid_ref[at]) + dot(pick, lo_ref[at]))

            left_e = le_ref[e]
        z = left_e + right
        group = (row_match & (col_edge == e)).astype(F32).astype(BF16)
        v_hi, v_lo = split(jnp.maximum(z, 0.2 * z) * att)
        score = score + (dot(v_hi, group) + dot(v_lo, group))
        p_hi, p_lo = split(g * left_e)
        dp = dp + (dot(p_hi, group) + dot(p_lo, group))

    spread = (lax.broadcasted_iota(jnp.int32, (DEG, LANES), 0)
              == ((lax.broadcasted_iota(jnp.int32, (DEG, LANES), 1) >> 3) & 7)).astype(F32)
    alive = dot((mask_ref[...].T > 0).astype(F32), spread) > 0.5

    def over_edges(x, op):
        for shift in (8, 16, 32):
            x = op(x, pltpu.roll(x, shift, 1))
        return x

    score = jnp.where(alive, score, -1e30)
    top = over_edges(score, jnp.maximum)
    weights = jnp.where(alive, jnp.exp(score - top), 0.0)
    prob = weights / over_edges(weights, jnp.add)
    ds = prob * (dp - over_edges(prob * dp, jnp.add))
    first_half = lax.broadcasted_iota(jnp.int32, (rows, LANES), 1) < LANES // 2

    def halves(x):
        hi = x.astype(BF16).astype(F32)
        return jnp.where(first_half, hi, x - hi).astype(BF16)

    prob_hl = halves(prob)
    ds_hl = halves(ds)

    krow = lax.broadcasted_iota(jnp.int32, (LANES, WIDTH), 0)
    kmatch = (krow & 7) == lax.broadcasted_iota(jnp.int32, (LANES, WIDTH), 1) // HD
    kedge = (krow >> 3) & 7
    out = jnp.zeros((rows, WIDTH), F32)
    d_right = jnp.zeros((rows, WIDTH), F32)
    d_att = jnp.zeros((8, WIDTH), F32)
    for e in range(DEG):
        widen = (kmatch & (kedge == e)).astype(F32).astype(BF16)
        prob_w = dot(prob_hl, widen)
        ds_w = dot(ds_hl, widen)
        left_e = le_ref[e]
        z = left_e + right
        slope = jnp.where(z > 0, 1.0, 0.2)
        out = out + prob_w * left_e
        t = ds_w * slope
        inner = t * att
        d_right = d_right + inner
        d_att = d_att + jnp.sum((t * z).reshape(rows // 8, 8, WIDTH), axis=0)
        dhi_ref[e * rows:(e + 1) * rows], dlo_ref[e * rows:(e + 1) * rows] = split(prob_w * g + inner)
    out_ref[...] = out

    slot_row = lax.broadcasted_iota(jnp.int32, (CHUNK, rows), 0)

    def scatter(c):
        total = jnp.zeros((CHUNK, WIDTH), F32)
        for e in range(DEG):
            put = (slot_row + c * CHUNK == slot_t[e:e + 1]).astype(F32).astype(BF16)
            total = total + (dot(put, dhi_ref[e * rows:(e + 1) * rows]) + dot(put, dlo_ref[e * rows:(e + 1) * rows]))
        return total

    if chunks == 1:
        d_left = scatter(0)
        ret_ref[...] = dot3(d_left, wl_ref[...], ((1,), (1,)))
        wg_ref[0:FI] = dot3(fetched_ref[...].T, d_left)
    else:
        wg_ref[0:FI] = jnp.zeros((FI, WIDTH), F32)

        @pl.loop(0, chunks)
        def _(c):
            at = pl.ds(pl.multiple_of(c * CHUNK, CHUNK), CHUNK)
            d_left = scatter(c)
            ret_ref[at] = dot3(d_left, wl_ref[...], ((1,), (1,)))
            wg_ref[0:FI] += dot3(fetched_ref[at].T, d_left)
    fg_ref[...] = dot3(d_right, wr_ref[...], ((1,), (1,)))
    wg_ref[FI:2 * FI] = dot3(feat_ref[...].T, d_right)

    unit, per = units(n)
    for u in range(n * per):
        rb, lb = u // 4, u % 4
        msg_ref[u // per, (u % per) * unit:(u % per + 1) * unit] = (
            wg_ref[rb * unit:(rb + 1) * unit, lb * LANES:(lb + 1) * LANES])
    att_row = jnp.sum(d_att, axis=0, keepdims=True)
    tail = jnp.concatenate([att_row[:, b * LANES:(b + 1) * LANES] for b in range(4)] + [jnp.zeros((4, LANES), F32)], axis=0)
    tail_ref[...] = tail


def units(n):
    unit = max(8, 2 * FI // n)
    return unit, (2 * FI // unit) * 4 // n


def levels(n):
    mid = 1
    while mid * mid * 4 <= n // 2:
        mid *= 2
    return n // 2 // mid, mid


def return_kernel(n, ret_ref, fg_ref, msg_ref, att_ref, asked_ref, fgo_ref, gl_ref, gr_ref, ga_ref,
                  ret_in, half_in, half, mid_in, part, outer_in, gathered, att_core, att_mid, att_outer,
                  ret_sems, sems, att_sems, chunk_sems, core_sems):
    me = lax.axis_index("row")
    outer, mid = levels(n)
    plane = mid * outer
    o, m, c = me // (2 * mid), lax.rem(me // 2, mid), lax.rem(me, 2)
    unit, per = units(n)
    barrier = pltpu.get_barrier_semaphore()

    def remote(src, dst, peer, sem, slot):
        return pltpu.make_async_remote_copy(
            src_ref=src, dst_ref=dst, send_sem=sem.at[0, slot], recv_sem=sem.at[1, slot],
            device_id={"row": peer}, device_id_type=MESH)

    def send_ret(k):
        peer = lax.rem(me + k, n)
        return remote(ret_ref.at[peer], ret_in.at[me], peer, ret_sems, k)

    def mid_peer(k):
        at = lax.rem(m + k, mid)
        return at, (o * mid + at) * 2 + c

    def outer_peer(k):
        at = lax.rem(o + k, outer)
        return at, (at * mid + m) * 2 + c

    partner = me + 1 - 2 * c
    first, second, third = 1, mid, mid + outer
    mine = pl.ds(c * plane, plane)
    spot = c * plane + m * outer + o

    greet(n, me, barrier)

    to_core = [
        remote(att_ref, att_core, partner, att_sems, 0),
        remote(msg_ref.at[pl.ds((1 - c) * plane, plane)], half_in, partner, sems, 0),
    ]
    for copy in to_core:
        copy.start()

    @pl.loop(1, n)
    def _(k):
        send_ret(k).start()

    ret_in[me] = ret_ref[me]
    for copy in to_core:
        copy.wait_recv()
    att_mid[m] = att_ref[...] + att_core[...]
    half[...] = msg_ref[mine] + half_in[...]

    to_mid = []
    for k in range(1, mid):
        to_mid.append(remote(att_mid.at[m], att_mid.at[m], mid_peer(k)[1], att_sems, first + k - 1))
    mid_chunks = []
    for j in list(range(1, outer)) + [0]:
        there = lax.rem(o + j, outer)
        mid_chunks.append((there, [
            remote(half.at[mid_peer(k)[0] * outer + there], mid_in.at[m, there], mid_peer(k)[1], chunk_sems, (k - 1) * outer + j)
            for k in range(1, mid)]))
    for copy in to_mid:
        copy.start()
    for _, copies in mid_chunks:
        for copy in copies:
            copy.start()
    for copy in to_mid:
        copy.wait_recv()
    att = att_mid[0]
    for k in range(1, mid):
        att = att + att_mid[k]
    att_outer[o] = att

    to_outer = [remote(att_outer.at[o], att_outer.at[o], outer_peer(k)[1], att_sems, second + k - 1)
                for k in range(1, outer)]
    for copy in to_outer:
        copy.start()
    for j, (there, copies) in enumerate(mid_chunks, 1):
        for copy in copies:
            copy.wait_recv()
        total = half[m * outer + there]
        for k in range(1, mid):
            total = total + mid_in[lax.rem(m + k, mid), there]
        part[there] = total
        if j < outer:
            copy = remote(part.at[there], outer_in.at[o], outer_peer(j)[1], sems, second + j - 1)
            copy.start()
            to_outer.append(copy)
    for copy in to_outer:
        copy.wait_recv()
    total = part[o]
    for k in range(1, outer):
        total = total + outer_in[lax.rem(o + k, outer)]
    gathered[spot] = total

    def place(km, j):
        return c * plane + lax.rem(m - km + mid, mid) * outer + lax.rem(o - j + outer, outer)

    def pass_core(km, j):
        at = gathered.at[place(km, j)]
        return remote(at, at, partner, core_sems, km * outer + j)

    def pass_mid(k, j):
        at = gathered.at[place(0, j)]
        return remote(at, at, mid_peer(k)[1], chunk_sems, (mid - 1) * outer + (k - 1) * outer + j)

    back_outer = [remote(gathered.at[spot], gathered.at[spot], outer_peer(k)[1], sems, third + k - 1)
                  for k in range(1, outer)]
    back_mid = [[pass_mid(k, j) for k in range(1, mid)] for j in range(outer)]
    back_core = {(km, j): pass_core(km, j) for km in range(mid) for j in range(outer)}
    for copy in back_outer + back_mid[0] + [back_core[0, 0]]:
        copy.start()
    att = att_outer[0]
    for k in range(1, outer):
        att = att + att_outer[k]
    for b in range(4):
        ga_ref[2 * b:2 * b + 1] = att[b:b + 1, :HD]
        ga_ref[2 * b + 1:2 * b + 2] = att[b:b + 1, HD:]
    for j in range(1, outer):
        back_outer[j - 1].wait_recv()
        for copy in back_mid[j] + [back_core[0, j]]:
            copy.start()
    for j in range(outer):
        for k in range(1, mid):
            back_mid[j][k - 1].wait_recv()
            back_core[k, j].start()

    @pl.loop(1, n)
    def _(k):
        send_ret(k).wait_recv()

    tiles = fg_ref.shape[0] // TILE

    def collect(q, acc):
        want = asked_ref[q]
        back = ret_in[q].reshape(TILE // 8, 8, FI)
        return tuple(acc[t] + jnp.where((want == t)[None], back, 0.0) for t in range(tiles))

    start = tuple(fg_ref[t * TILE:(t + 1) * TILE].reshape(TILE // 8, 8, FI) for t in range(tiles))
    done = lax.fori_loop(0, n, collect, start)
    for t in range(tiles):
        fgo_ref[t * TILE:(t + 1) * TILE] = done[t].reshape(TILE, FI)

    for copy in back_core.values():
        copy.wait_recv()

    for u in range(n * per):
        rb, lb = u // 4, u % 4
        ref, base = (gl_ref, 0) if rb * unit < FI else (gr_ref, FI)
        ref[rb * unit - base:(rb + 1) * unit - base, lb * LANES:(lb + 1) * LANES] = (
            gathered[u // per, (u % per) * unit:(u % per + 1) * unit])

    passed = [copy for _, copies in mid_chunks for copy in copies] + [copy for copies in back_mid for copy in copies]
    for copy in to_core + to_mid + to_outer + back_outer + passed + list(back_core.values()):
        copy.wait_send()

    @pl.loop(1, n)
    def _(k):
        send_ret(k).wait_send()


def on_device(features, w_left, w_right, attention, requests, src_slot, edge_mask, g_out):
    n = lax.axis_size("row")
    rows = features.shape[0]
    vmem = pl.BlockSpec(memory_space=pltpu.VMEM)
    smem = pl.BlockSpec(memory_space=pltpu.SMEM)
    limit = 56 * 2**20 if n > 16 else 40 * 2**20

    def shape(*dims, kind=F32):
        return jax.ShapeDtypeStruct(dims, kind)

    fetched, asked = pl.pallas_call(
        functools.partial(fetch_kernel, n),
        out_shape=(shape(n * TILE, FI), shape(n, 8, LANES, kind=jnp.int32)),
        in_specs=[smem, vmem],
        out_specs=(vmem, vmem),
        scratch_shapes=[
            pltpu.VMEM((n, 8, LANES), jnp.int32),
            pltpu.VMEM((n, TILE, FI), F32),
            pltpu.VMEM((n, 8, LANES), jnp.int32),
            pltpu.VMEM((n, TILE, FI), F32),
            pltpu.SemaphoreType.DMA((4, n)),
        ],
        compiler_params=pltpu.CompilerParams(collective_id=0, has_side_effects=True, vmem_limit_bytes=limit),
        cost_estimate=pl.CostEstimate(flops=12 * 10**9, bytes_accessed=48 * 2**20, transcendentals=0),
        name="fetch",
    )(requests, features)

    unit, per = units(n)
    body = unit * per
    outer, mid = levels(n)
    out, ret, fg, msg, tail = pl.pallas_call(
        functools.partial(local_kernel, n),
        out_shape=(shape(rows, WIDTH), shape(n * TILE, FI), shape(rows, FI), shape(n, body, LANES), shape(8, LANES)),
        in_specs=[vmem] * 8,
        out_specs=(vmem,) * 5,
        scratch_shapes=[
            pltpu.VMEM((n * TILE, WIDTH), BF16),
            pltpu.VMEM((n * TILE, WIDTH), BF16),
            pltpu.VMEM((n * TILE, WIDTH), BF16),
            pltpu.VMEM((DEG, rows, WIDTH), F32),
            pltpu.VMEM((DEG * rows, WIDTH), BF16),
            pltpu.VMEM((DEG * rows, WIDTH), BF16),
            pltpu.VMEM((2 * FI, WIDTH), F32),
        ],
        compiler_params=pltpu.CompilerParams(vmem_limit_bytes=limit),
        cost_estimate=pl.CostEstimate(flops=12 * 10**9, bytes_accessed=4 * 2**20, transcendentals=0),
        name="local",
    )(fetched, features, w_left, w_right, attention, src_slot.T, edge_mask.T, g_out)

    feature_gradient, grad_left, grad_right, grad_att = pl.pallas_call(
        functools.partial(return_kernel, n),
        out_shape=(shape(rows, FI), shape(FI, WIDTH), shape(FI, WIDTH), shape(HEADS, HD)),
        in_specs=[vmem] * 5,
        out_specs=(vmem,) * 4,
        scratch_shapes=[
            pltpu.VMEM((n, TILE, FI), F32),
            pltpu.VMEM((outer * mid, body, LANES), F32),
            pltpu.VMEM((outer * mid, body, LANES), F32),
            pltpu.VMEM((mid, outer, body, LANES), F32),
            pltpu.VMEM((outer, body, LANES), F32),
            pltpu.VMEM((outer, body, LANES), F32),
            pltpu.VMEM((n, body, LANES), F32),
            pltpu.VMEM((8, LANES), F32),
            pltpu.VMEM((mid, 8, LANES), F32),
            pltpu.VMEM((outer, 8, LANES), F32),
            pltpu.SemaphoreType.DMA((2, n)),
            pltpu.SemaphoreType.DMA((2, 2 * (outer + mid))),
            pltpu.SemaphoreType.DMA((2, outer + mid)),
            pltpu.SemaphoreType.DMA((2, 2 * mid * outer)),
            pltpu.SemaphoreType.DMA((2, mid * outer)),
        ],
        compiler_params=pltpu.CompilerParams(collective_id=1, has_side_effects=True, vmem_limit_bytes=limit),
        name="give_back",
    )(ret.reshape(n, TILE, FI), fg, msg, tail, asked)
    return (out, feature_gradient, grad_left, grad_right, grad_att)


def solution(mesh):
    rowwise = P(("group", "row"), None)
    in_specs = (rowwise, P(), P(), P(), rowwise, rowwise, rowwise, rowwise)
    out_specs = (rowwise, rowwise, P("group", None), P("group", None), P("group", None))
    return jax.shard_map(
        on_device, mesh=mesh, in_specs=in_specs, out_specs=out_specs, check_vma=False
    )
```
